32 devices in a mesh: section: 2 (over core), seq: 4 (over z), wa: 4 (over y, x).
Axes of the slice: x: 2, y: 2, z: 4, core: 2. Of those that a mesh axis runs over, the one named last changes fastest.
Arguments:
- tokens: bfloat16 [2, 4, 2048, 1024], P(None, 'wa', 'seq'), may hold values from -6 to 6
- cotangent: bfloat16 [2, 4, 2048, 1024], P(None, 'wa', 'seq'), may hold values from -6 to 6
- input_gain: bfloat16 [2, 1024], P('section', 'wa'), may hold values from 0.25 to 1.75
- gate_proj: bfloat16 [2, 1024, 2048], P('section', 'wa'), may hold values from -0.1875 to 0.1875
- mixed_proj: bfloat16 [2, 1024, 2304], P('section', 'wa'), may hold values from -0.1875 to 0.1875
- step_proj: bfloat16 [2, 1024, 32], P('section', 'wa'), may hold values from -0.1875 to 0.1875
- conv_kernel: bfloat16 [2, 4, 2304], P('section', None, 'wa'), may hold values from -3 to 3
- conv_bias: bfloat16 [2, 2304], P('section', 'wa'), may hold values from -3 to 3
- step_bias: bfloat16 [2, 32], P('section', 'wa'), may hold values from -16 to -2, as said below
- decay_log: bfloat16 [2, 32], P('section', 'wa'), may hold values from 0 to 1.1953125
- skip_gain: bfloat16 [2, 32], P('section', 'wa'), may hold values from 0.5 to 1.5
- output_gain: bfloat16 [2, 2048], P('section', 'wa'), may hold values from 0.25 to 1.75
- out_proj: bfloat16 [2, 2048, 1024], P('section', 'wa'), may hold values from -0.125 to 0.125
Outputs:
- layer_out: bfloat16 [2, 2, 4, 2048, 1024], P('section', None, 'wa', 'seq')
- input_grad: float32 [2, 2, 4, 2048, 1024], P('section', None, 'wa', 'seq')
- input_gain_grad: float32 [2, 1024], P('section', 'wa')
- gate_proj_grad: float32 [2, 1024, 2048], P('section', 'wa')
- mixed_proj_grad: float32 [2, 1024, 2304], P('section', 'wa')
- step_proj_grad: float32 [2, 1024, 32], P('section', 'wa')
- conv_kernel_grad: float32 [2, 4, 2304], P('section', None, 'wa')
- conv_bias_grad: float32 [2, 2304], P('section', 'wa')
- step_bias_grad: float32 [2, 32], P('section', 'wa')
- decay_log_grad: float32 [2, 32], P('section', 'wa')
- skip_gain_grad: float32 [2, 32], P('section', 'wa')
- output_gain_grad: float32 [2, 2048], P('section', 'wa')
- out_proj_grad: float32 [2, 2048, 1024], P('section', 'wa')
The draws below stay inside these ranges and needn't reach their ends.
Inputs may be any that keep to these rules, and one draw needn't show every extreme that they name: `step_bias`: a per-head number; softplus of it lies between about 0.02 / 2048 and about 0.05.
All inputs are finite; a program needn't handle non-finite values.
Results may differ from the reference program's by a relative error of at most 0.035.
Values may be sent and summed in bfloat16 or wider, within the bound.
A program may use at most 448 MiB of HBM per device.

```python
import jax
import jax.numpy as jnp
from jax import lax

D = 1024
DI = 2048
NHEADS = 32
HEADDIM = 64
KERNEL = 4
GROUP = 256
MICRO = 2
NCONV = 2304
LENGTH = 2048
BATCH = 4
LAYERS = 2


def draw_step_bias(key, part):
    key = jax.random.fold_in(key, 7)
    pick_key, slow_key, fast_key = jax.random.split(key, 3)
    share = 0.55
    slow_mask = jax.random.uniform(pick_key, (LAYERS, NHEADS)) < share
    slow_log = jax.random.uniform(slow_key, (LAYERS, NHEADS), minval=jnp.log(0.02 / LENGTH), maxval=jnp.log(0.3 / LENGTH))
    fast_log = jax.random.uniform(fast_key, (LAYERS, NHEADS), minval=jnp.log(0.01), maxval=jnp.log(0.05))
    rates = jnp.exp(jnp.where(slow_mask, slow_log, fast_log))
    return jnp.log(jnp.expm1(rates)).astype(jnp.bfloat16)


def block_scale(rng, dims, cuts, least, largest):
    loudness = 1.0
    for axis_at, shards_of in cuts:
        heights = jax.random.uniform(jax.random.fold_in(jax.random.fold_in(rng, 6), axis_at), (shards_of,), jnp.float32, least / len(cuts), largest / len(cuts))
        loudness = loudness * jnp.repeat(jnp.exp(heights), dims[axis_at] // shards_of).reshape((-1,) + (1,) * (len(dims) - 1 - axis_at))
    return loudness


def noise(rng, extent, scale, reach, cuts=(), dtype=jnp.bfloat16):
    loudness = block_scale(rng, extent, cuts, -0.22, 0.18) if cuts else 1.0
    values = jax.random.normal(rng, extent, jnp.float32) * scale * loudness
    return jnp.minimum(jnp.maximum(values, -reach), reach).astype(dtype)


def setup_inputs(seed: int = 0) -> dict:
    splits = jax.random.split(jax.random.key(seed), 14)
    return {
        "tokens": noise(splits[0], (MICRO, BATCH, LENGTH, D), 1.0, 6.0, ((1, 4), (2, 4))),
        "cotangent": noise(splits[1], (MICRO, BATCH, LENGTH, D), 1.0, 6.0, ((1, 4), (2, 4))),
        "input_gain": jnp.clip(1.0 + 0.15 * jax.random.normal(splits[2], (LAYERS, D), jnp.float32), 0.25, 1.75).astype(jnp.bfloat16),
        "gate_proj": noise(splits[3], (LAYERS, D, DI), D ** -0.5, 0.1875, ((0, 2), (1, 4))),
        "mixed_proj": noise(splits[4], (LAYERS, D, NCONV), D ** -0.5, 0.1875, ((0, 2), (1, 4))),
        "step_proj": noise(splits[5], (LAYERS, D, NHEADS), D ** -0.5, 0.1875, ((0, 2), (1, 4))),
        "conv_kernel": noise(splits[6], (LAYERS, KERNEL, NCONV), KERNEL ** -0.5, 3.0, ((0, 2), (2, 4))),
        "conv_bias": noise(splits[7], (LAYERS, NCONV), 0.5, 3.0, ((0, 2), (1, 4))),
        "step_bias": draw_step_bias(jax.random.fold_in(splits[13], 71), 0),
        "decay_log": jnp.clip(1.1953125 * jax.random.uniform(splits[9], (LAYERS, NHEADS), jnp.float32) ** block_scale(splits[9], (LAYERS, NHEADS), ((0, 2), (1, 4)), -0.2, 0.2), 0.0, 1.1953125).astype(jnp.bfloat16),
        "skip_gain": jnp.clip(0.5 + 1.0 * jax.random.uniform(splits[10], (LAYERS, NHEADS), jnp.float32) ** block_scale(splits[10], (LAYERS, NHEADS), ((0, 2), (1, 4)), -0.2, 0.2), 0.5, 1.5).astype(jnp.bfloat16),
        "output_gain": jnp.clip(1.0 + 0.15 * jax.random.normal(splits[11], (LAYERS, DI), jnp.float32), 0.25, 1.75).astype(jnp.bfloat16),
        "out_proj": noise(splits[12], (LAYERS, DI, D), DI ** -0.5, 0.125, ((0, 2), (1, 4))),
    }


@jax.custom_vjp
def low(v):
    return lax.optimization_barrier(v.astype(jnp.bfloat16)).astype(jnp.float32)

@jax.custom_vjp
def low_back(v):
    return v

def low_keep(v):
    return (low(v), None)

def low_pass(kept, grad):
    return (grad,)

def back_keep(v):
    return (v, None)

def back_low(kept, grad):
    return (low(grad),)
low.defvjp(low_keep, low_pass)
low_back.defvjp(back_keep, back_low)
EPSILON = 1e-05
HIGHEST = lax.Precision.HIGHEST

def rms_scale(values, gain):
    return values * lax.rsqrt(lax.optimization_barrier(jnp.mean(values * values, axis=-1, keepdims=True)) + EPSILON) * gain

def ssd_block(state_in, pieces):
    log_decay, time_step, values, keys_in, queries = pieces
    seq_count, length, head_count = log_decay.shape
    cumulative = jnp.cumsum(log_decay, axis=1)
    gram_mat = jnp.einsum('btn,bsn->bts', queries, keys_in, precision=HIGHEST)
    spread = cumulative[:, :, None, :] - cumulative[:, None, :, :]
    lower_mask = (jnp.arange(length)[:, None] >= jnp.arange(length)[None, :])[None, :, :, None]
    decay_mat = jnp.where(lower_mask, jnp.exp(jnp.where(lower_mask, spread, 0.0)), 0.0)
    mixing = low(gram_mat[:, :, :, None] * decay_mat * time_step[:, None, :, :])
    per_head = values.reshape(seq_count, length, head_count, HEADDIM)
    inner_part = low_back(jnp.einsum('btsh,bshp->bthp', mixing, per_head, precision=HIGHEST).reshape(seq_count, length, head_count * HEADDIM))
    reach_mat = jnp.einsum('btn,bdn->btd', queries, state_in, precision=HIGHEST)
    outer_part = reach_mat * jnp.repeat(jnp.exp(cumulative), HEADDIM, axis=2)
    weight = jnp.exp(cumulative[:, -1:, :] - cumulative) * time_step
    scaled = values * jnp.repeat(weight, HEADDIM, axis=2)
    fresh_state = jnp.einsum('bsd,bsn->bdn', scaled, keys_in, precision=HIGHEST)
    carried = state_in * jnp.repeat(jnp.exp(cumulative[:, -1, :]), HEADDIM, axis=1)[:, :, None] + fresh_state
    return (carried, inner_part + outer_part)

def layer(hidden, params):
    input_gain, gate_proj, mixed_proj, step_proj, conv_kernel, conv_bias, step_bias, decay_log, skip_gain, output_gain, out_proj = params
    seq_count, length, width = hidden.shape
    inner_width = gate_proj.shape[1]
    state_width = (mixed_proj.shape[1] - inner_width) // 2
    normed = low(rms_scale(hidden, input_gain))
    gate_pre = low_back(jnp.einsum('bld,de->ble', normed, gate_proj, precision=HIGHEST))
    mixed = low(low_back(jnp.einsum('bld,de->ble', normed, mixed_proj, precision=HIGHEST)))
    step_raw = low_back(jnp.einsum('bld,de->ble', normed, step_proj, precision=HIGHEST))
    padded = jnp.pad(mixed, ((0, 0), (KERNEL - 1, 0), (0, 0)))
    conv_sum = conv_bias
    for offset in range(KERNEL):
        conv_sum = conv_sum + conv_kernel[offset] * padded[:, offset:offset + length]
    active = low(jax.nn.silu(conv_sum))
    time_step = jax.nn.softplus(step_raw + step_bias)
    log_decay = -jnp.exp(decay_log) * time_step
    values = active[:, :, :inner_width]
    keys_in = active[:, :, inner_width:inner_width + state_width]
    queries = active[:, :, inner_width + state_width:]
    block_count = length // GROUP

    def split_blocks(array):
        return jnp.moveaxis(array.reshape(seq_count, block_count, GROUP, array.shape[-1]), 1, 0)
    start_state = jnp.zeros((seq_count, inner_width, state_width), jnp.float32)
    final_state, outputs = lax.scan(jax.checkpoint(ssd_block), start_state, (split_blocks(log_decay), split_blocks(time_step), split_blocks(values), split_blocks(keys_in), split_blocks(queries)))
    ssm_out = jnp.moveaxis(outputs, 0, 1).reshape(seq_count, length, inner_width)
    mixed_out = ssm_out + values * jnp.repeat(skip_gain, HEADDIM)
    normed_out = low(rms_scale(mixed_out * jax.nn.silu(gate_pre), output_gain))
    projected = low_back(jnp.einsum('ble,ed->bld', normed_out, out_proj, precision=HIGHEST))
    return low(hidden + projected)

def run_layer(inputs, *params):
    return layer(inputs, params)

def reference(tokens, cotangent, input_gain, gate_proj, mixed_proj, step_proj, conv_kernel, conv_bias, step_bias, decay_log, skip_gain, output_gain, out_proj):
    weights = (input_gain, gate_proj, mixed_proj, step_proj, conv_kernel, conv_bias, step_bias, decay_log, skip_gain, output_gain, out_proj)
    floats = tuple((item.astype(jnp.float32) for item in weights))
    seq_total = MICRO * BATCH
    current = tokens.astype(jnp.float32).reshape(seq_total, LENGTH, D)
    outs_list = []
    backs = []
    for level in range(LAYERS):
        params = tuple((item[level] for item in floats))
        current, back_fn = jax.vjp(run_layer, current, *params)
        outs_list.append(current)
        backs.append(back_fn)
    grad_now = cotangent.astype(jnp.float32).reshape(seq_total, LENGTH, D)
    input_list = [None] * LAYERS
    param_list = [None] * LAYERS
    for level in reversed(range(LAYERS)):
        results = backs[level](grad_now)
        grad_now = results[0]
        input_list[level] = grad_now
        param_list[level] = results[1:]
    full_shape = (LAYERS, MICRO, BATCH, LENGTH, D)
    layer_out = jnp.stack(outs_list).reshape(full_shape).astype(jnp.bfloat16)
    input_grad = jnp.stack(input_list).reshape(full_shape)
    grads = [jnp.stack([param_list[level][number] for level in range(LAYERS)]) for number in range(11)]
    return (layer_out, input_grad, grads[0], grads[1], grads[2], grads[3], grads[4], grads[5], grads[6], grads[7], grads[8], grads[9], grads[10])
```

```python
import jax
import jax.numpy as jnp
from jax import lax
from jax.sharding import PartitionSpec as P

HEADDIM = 64
GROUP = 128


EPSILON = 1e-05
HIGHEST = lax.Precision.DEFAULT


def passed_along(block, axis, distance):
    devices = range(lax.axis_size(axis))
    route = [(i - distance, i) for i in devices if i - distance in devices]
    return lax.ppermute(block, axis, route)


def rms_scale(values, gain):
    return values * lax.rsqrt(jnp.mean(values * values, axis=-1, keepdims=True) + EPSILON) * gain


def expand_heads(decays):
    return jnp.repeat(decays, HEADDIM, axis=-1)[..., None]


def join_states(earlier, later):
    return (earlier[0] * later[0], earlier[1] * expand_heads(later[0]) + later[1])


def entry_piece(hidden, input_gain):
    return rms_scale(hidden, input_gain)


def conv_piece(extended, step_raw, conv_kernel, conv_bias, step_bias, decay_log):
    length = step_raw.shape[0]
    conv_sum = conv_bias
    for offset in range(conv_kernel.shape[0]):
        conv_sum = conv_sum + conv_kernel[offset] * extended[offset : offset + length]
    time_step = jax.nn.softplus(step_raw + step_bias)
    return (jax.nn.silu(conv_sum), time_step, -jnp.exp(decay_log) * time_step)


def block_piece(log_decay, time_step, values, keys_in, queries):
    length = log_decay.shape[0]
    cumulative = jnp.cumsum(log_decay, axis=0)
    gram_mat = jnp.einsum("tn,sn->ts", queries, keys_in, precision=HIGHEST)
    by_head = cumulative.T
    spread = by_head[:, :, None] - by_head[:, None, :]
    lower_mask = (jnp.arange(length)[:, None] >= jnp.arange(length)[None, :])[None]
    decay_mat = jnp.where(lower_mask, jnp.exp(jnp.where(lower_mask, spread, 0.0)), 0.0)
    mixing = gram_mat[None] * decay_mat * time_step.T[:, None, :]
    weight = jnp.exp(cumulative[-1:] - cumulative) * time_step
    scaled = values * jnp.repeat(weight, HEADDIM, axis=1)
    fresh_state = jnp.einsum("sd,sn->dn", scaled, keys_in, precision=HIGHEST)
    return (mixing, fresh_state, jnp.exp(cumulative[-1]), jnp.exp(cumulative))


def reach_piece(growth, queries, start_state):
    reach_mat = jnp.einsum("tn,dn->td", queries, start_state, precision=HIGHEST)
    return reach_mat * jnp.repeat(growth, HEADDIM, axis=1)


def own_piece(fresh_all, decay_all):
    own_state = jnp.zeros_like(fresh_all[0])
    own_decay = jnp.ones_like(decay_all[0])
    prefixes = []
    prefix_decay = []
    for block_index in range(fresh_all.shape[0]):
        prefixes.append(own_state)
        prefix_decay.append(own_decay)
        own_state = own_state * expand_heads(decay_all[block_index]) + fresh_all[block_index]
        own_decay = own_decay * decay_all[block_index]
    return (own_state, own_decay, jnp.stack(prefixes), jnp.stack(prefix_decay))


def start_piece(incoming, prefix_decay, prefixes):
    return incoming[None] * expand_heads(prefix_decay) + prefixes


def exit_piece(inner_all, outer_all, values, skip_gain, gate_pre, output_gain):
    mixed_out = inner_all + outer_all + values * jnp.repeat(skip_gain, HEADDIM)
    return rms_scale(mixed_out * jax.nn.silu(gate_pre), output_gain)


def to_other(block):
    count = lax.axis_size("section")
    return lax.ppermute(block, "section", [(i, (i + 1) % count) for i in range(count)])


def spread_states(state, decay):
    high = decay.astype(jnp.bfloat16)
    low = (decay - high.astype(jnp.float32)).astype(jnp.bfloat16)
    width = state.shape[1]
    heads = decay.shape[0]
    row = jnp.concatenate([high, low, jnp.zeros((width - 2 * heads,), jnp.bfloat16)])[None]
    packed = jnp.concatenate(
        [state.astype(jnp.bfloat16), row, jnp.zeros((15, width), jnp.bfloat16)], axis=0
    )
    gathered = lax.all_gather(packed, "seq")
    states = gathered[:, : state.shape[0]]
    parts = gathered[:, state.shape[0], : 2 * heads].astype(jnp.float32)
    return states, parts[:, :heads] + parts[:, heads:]


def carried_from(states, decays, ahead):
    count = lax.axis_size("seq")
    place = lax.axis_index("seq")
    source = jnp.arange(count)[:, None, None]
    middle = jnp.arange(count)[None, :, None]
    if ahead:
        between = jnp.logical_and(middle < source, middle > place)
        keep = jnp.arange(count) > place
    else:
        between = jnp.logical_and(middle > source, middle < place)
        keep = jnp.arange(count) < place
    factor = jnp.prod(jnp.where(between, decays[None], 1.0), axis=1)
    factor = jnp.where(keep[:, None], factor, 0.0)
    factor = jnp.repeat(factor, HEADDIM, axis=1)
    total = states[0].astype(jnp.float32) * factor[0][:, None]
    for index in range(1, count):
        total = total + states[index].astype(jnp.float32) * factor[index][:, None]
    return total


def layer_pass(hidden, params):
    (
        input_gain,
        gate_proj,
        mixed_proj,
        step_proj,
        conv_kernel,
        conv_bias,
        step_bias,
        decay_log,
        skip_gain,
        output_gain,
        out_proj,
    ) = params
    length = hidden.shape[0]
    inner_width = gate_proj.shape[1]
    state_width = (mixed_proj.shape[1] - inner_width) // 2
    head_count = step_proj.shape[1]
    block_count = length // GROUP
    rim_rows = conv_kernel.shape[0] - 1
    normed, entry_back = jax.vjp(entry_piece, hidden, input_gain.astype(jnp.float32))
    normed_low = normed.astype(jnp.bfloat16)
    gate_pre = jnp.dot(normed_low, gate_proj, preferred_element_type=jnp.float32)
    mixed_low = jnp.dot(normed_low, mixed_proj, preferred_element_type=jnp.float32).astype(
        jnp.bfloat16
    )
    step_raw = jnp.dot(normed_low, step_proj, preferred_element_type=jnp.float32)
    rim_in = passed_along(mixed_low[length - rim_rows :], "seq", 1)
    extended = jnp.concatenate([rim_in, mixed_low], axis=0).astype(jnp.float32)
    conv_out, conv_back = jax.vjp(
        conv_piece,
        extended,
        step_raw,
        conv_kernel.astype(jnp.float32),
        conv_bias.astype(jnp.float32),
        step_bias.astype(jnp.float32),
        decay_log.astype(jnp.float32),
    )
    active, time_step, log_decay = conv_out
    active_low = active.astype(jnp.bfloat16)
    active_up = active_low.astype(jnp.float32)
    values_low = active_low[:, :inner_width]
    values_up = active_up[:, :inner_width]
    keys_up = active_up[:, inner_width : inner_width + state_width]
    queries_up = active_up[:, inner_width + state_width :]
    inner_parts = []
    mixing_list = []
    block_backs = []
    fresh_list = []
    decay_list = []
    growth_list = []
    for block_index in range(block_count):
        row_span = slice(block_index * GROUP, (block_index + 1) * GROUP)
        outputs, block_back = jax.vjp(
            block_piece,
            log_decay[row_span],
            time_step[row_span],
            values_up[row_span],
            keys_up[row_span],
            queries_up[row_span],
        )
        mixing_low = outputs[0].astype(jnp.bfloat16)
        heads_view = values_low[row_span].reshape(GROUP, head_count, HEADDIM)
        inner_parts.append(
            jnp.einsum(
                "hts,shp->thp", mixing_low, heads_view, preferred_element_type=jnp.float32
            ).reshape(GROUP, inner_width)
        )
        mixing_list.append(mixing_low)
        block_backs.append(block_back)
        fresh_list.append(outputs[1])
        decay_list.append(outputs[2])
        growth_list.append(outputs[3])
    own_out, own_back = jax.vjp(own_piece, jnp.stack(fresh_list), jnp.stack(decay_list))
    own_state, own_decay, prefixes, prefix_decay = own_out
    states_all, decays_all = spread_states(own_state, own_decay)
    incoming = carried_from(states_all, decays_all, False)
    starts, start_back = jax.vjp(start_piece, incoming, prefix_decay, prefixes)
    outer_parts = []
    reach_backs = []
    for block_index in range(block_count):
        row_span = slice(block_index * GROUP, (block_index + 1) * GROUP)
        outer_part, reach_back = jax.vjp(
            reach_piece, growth_list[block_index], queries_up[row_span], starts[block_index]
        )
        outer_parts.append(outer_part)
        reach_backs.append(reach_back)
    inner_all = jnp.concatenate(inner_parts, axis=0)
    outer_all = jnp.concatenate(outer_parts, axis=0)
    normed_out, exit_back = jax.vjp(
        exit_piece,
        inner_all,
        outer_all,
        values_up,
        skip_gain.astype(jnp.float32),
        gate_pre,
        output_gain.astype(jnp.float32),
    )
    normed_out_low = normed_out.astype(jnp.bfloat16)
    result = hidden + jnp.dot(normed_out_low, out_proj, preferred_element_type=jnp.float32)
    tape = (
        normed_low,
        entry_back,
        conv_back,
        values_low,
        mixing_list,
        block_backs,
        own_back,
        decays_all,
        incoming,
        start_back,
        reach_backs,
        exit_back,
        normed_out_low,
    )
    return (result, tape)


def layer_back(grad_out, params, tape):
    (
        input_gain,
        gate_proj,
        mixed_proj,
        step_proj,
        conv_kernel,
        conv_bias,
        step_bias,
        decay_log,
        skip_gain,
        output_gain,
        out_proj,
    ) = params
    (
        normed_low,
        entry_back,
        conv_back,
        values_low,
        mixing_list,
        block_backs,
        own_back,
        decays_all,
        incoming,
        start_back,
        reach_backs,
        exit_back,
        normed_out_low,
    ) = tape
    length = grad_out.shape[0]
    inner_width = gate_proj.shape[1]
    head_count = step_proj.shape[1]
    block_count = length // GROUP
    rim_rows = conv_kernel.shape[0] - 1
    grad_proj = grad_out.astype(jnp.bfloat16)
    out_proj_grad = jnp.einsum(
        "te,td->ed", normed_out_low, grad_proj, preferred_element_type=jnp.float32
    )
    grad_normed_out = jnp.einsum(
        "td,ed->te", grad_proj, out_proj, preferred_element_type=jnp.float32
    )
    grad_inner, grad_outer, grad_values_skip, skip_gain_grad, grad_gate_pre, output_gain_grad = (
        exit_back(grad_normed_out)
    )
    grad_inner_low = grad_inner.astype(jnp.bfloat16)
    grad_mixings = []
    grad_values_inner = []
    grad_growths = []
    grad_queries_outer = []
    grad_starts = []
    for block_index in range(block_count):
        row_span = slice(block_index * GROUP, (block_index + 1) * GROUP)
        grad_heads = grad_inner_low[row_span].reshape(GROUP, head_count, HEADDIM)
        heads_view = values_low[row_span].reshape(GROUP, head_count, HEADDIM)
        grad_mixings.append(
            jnp.einsum("thp,shp->hts", grad_heads, heads_view, preferred_element_type=jnp.float32)
        )
        grad_values_inner.append(
            jnp.einsum(
                "hts,thp->shp",
                mixing_list[block_index],
                grad_heads,
                preferred_element_type=jnp.float32,
            ).reshape(GROUP, inner_width)
        )
        grad_growth, grad_query, grad_start = reach_backs[block_index](grad_outer[row_span])
        grad_growths.append(grad_growth)
        grad_queries_outer.append(grad_query)
        grad_starts.append(grad_start)
    grad_incoming, grad_prefix_decay, grad_prefixes = start_back(jnp.stack(grad_starts))
    adjoints = lax.all_gather(grad_incoming.astype(jnp.bfloat16), "seq")
    returned = carried_from(adjoints, decays_all, True)
    grad_own_decay = jnp.sum(returned * incoming, axis=1).reshape(head_count, HEADDIM).sum(axis=1)
    grad_fresh, grad_decays = own_back((returned, grad_own_decay, grad_prefixes, grad_prefix_decay))
    grad_log_list = []
    grad_step_list = []
    grad_values_list = []
    grad_keys_list = []
    grad_queries_list = []
    for block_index in range(block_count):
        grad_log, grad_step, grad_values, grad_keys, grad_queries = block_backs[block_index](
            (
                grad_mixings[block_index],
                grad_fresh[block_index],
                grad_decays[block_index],
                grad_growths[block_index],
            )
        )
        grad_log_list.append(grad_log)
        grad_step_list.append(grad_step)
        grad_values_list.append(grad_values + grad_values_inner[block_index])
        grad_keys_list.append(grad_keys)
        grad_queries_list.append(grad_queries + grad_queries_outer[block_index])
    grad_active = jnp.concatenate(
        [
            jnp.concatenate(grad_values_list, axis=0) + grad_values_skip,
            jnp.concatenate(grad_keys_list, axis=0),
            jnp.concatenate(grad_queries_list, axis=0),
        ],
        axis=1,
    )
    (
        grad_extended,
        grad_step_raw,
        conv_kernel_grad,
        conv_bias_grad,
        step_bias_grad,
        decay_log_grad,
    ) = conv_back(
        (
            grad_active,
            jnp.concatenate(grad_step_list, axis=0),
            jnp.concatenate(grad_log_list, axis=0),
        )
    )
    back_rim = passed_along(grad_extended[:rim_rows], "seq", -1)
    grad_mixed = grad_extended[rim_rows:] + jnp.pad(back_rim, ((length - rim_rows, 0), (0, 0)))
    grad_gate_low = grad_gate_pre.astype(jnp.bfloat16)
    grad_mixed_low = grad_mixed.astype(jnp.bfloat16)
    grad_step_low = grad_step_raw.astype(jnp.bfloat16)
    gate_proj_grad = jnp.einsum(
        "td,te->de", normed_low, grad_gate_low, preferred_element_type=jnp.float32
    )
    mixed_proj_grad = jnp.einsum(
        "td,te->de", normed_low, grad_mixed_low, preferred_element_type=jnp.float32
    )
    step_proj_grad = jnp.einsum(
        "td,te->de", normed_low, grad_step_low, preferred_element_type=jnp.float32
    )
    grad_normed = jnp.einsum(
        "te,de->td", grad_gate_low, gate_proj, preferred_element_type=jnp.float32
    )
    grad_normed = grad_normed + jnp.einsum(
        "te,de->td", grad_mixed_low, mixed_proj, preferred_element_type=jnp.float32
    )
    grad_normed = grad_normed + jnp.einsum(
        "te,de->td", grad_step_low, step_proj, preferred_element_type=jnp.float32
    )
    grad_hidden, input_gain_grad = entry_back(grad_normed)
    grads = (
        input_gain_grad,
        gate_proj_grad,
        mixed_proj_grad,
        step_proj_grad,
        conv_kernel_grad,
        conv_bias_grad,
        step_bias_grad,
        decay_log_grad,
        skip_gain_grad,
        output_gain_grad,
        out_proj_grad,
    )
    return (grad_out + grad_hidden, grads)


SMALL = ((0, 1), (3, 1), (4, 2), (5, 1), (6, 1), (7, 1), (8, 1), (9, 1))
LARGE = (2, 1, 10)


def fetch_small(shards):
    flat = jnp.concatenate([shards[at].reshape(-1) for at, _ in SMALL])
    gathered = lax.all_gather(flat, ("section", "wa"))
    sections = lax.axis_size("section")
    count = lax.axis_size("wa")
    gathered = gathered.reshape(sections, count, -1)
    layers = []
    for level in range(sections):
        whole = {}
        start = 0
        for at, axis in SMALL:
            shape = shards[at].shape[1:]
            size = shards[at][0].size
            part = gathered[level, :, start : start + size]
            start += size
            part = part.reshape((count,) + shape)
            if axis == 1:
                whole[at] = part.reshape((count * shape[0],) + shape[1:])
            else:
                whole[at] = jnp.moveaxis(part, 0, 1).reshape((shape[0], count * shape[1]))
        layers.append(whole)
    return layers


def fetch_large(shards):
    sections = lax.axis_size("section")
    rank = lax.axis_index("section")
    mine = {at: shards[at][0] for at in LARGE}
    layers = [dict() for _ in range(sections)]
    for at in LARGE:
        rows, columns = mine[at].shape
        cut = mine[at].reshape(sections, rows // sections, columns)
        pieces = swapped(cut, rank, sections)
        for level in range(sections):
            layers[level][at] = lax.all_gather(
                pieces[level], ("wa", "section"), axis=0, tiled=True
            )
    return layers


def swapped(cut, rank, sections):
    got = [None] * sections
    arrivals = [lax.dynamic_index_in_dim(cut, rank, 0, False)]
    for hop in range(1, sections):
        target = lax.rem(rank + hop, sections)
        block = lax.dynamic_index_in_dim(cut, target, 0, False)
        arrivals.append(
            lax.ppermute(block, "section", [(i, (i + hop) % sections) for i in range(sections)])
        )
    for level in range(sections):
        value = arrivals[0]
        for hop in range(1, sections):
            value = jnp.where(lax.rem(level + hop, sections) == rank, arrivals[hop], value)
        got[level] = value
    return got


def scatter_large(grad):
    return lax.psum_scatter(
        grad.astype(jnp.bfloat16), ("wa", "section"), scatter_dimension=0, tiled=True
    )


def reduce_small(grads):
    flat = jnp.concatenate([grads[at].reshape(-1) for at, _ in SMALL])
    return lax.psum(flat, ("section", "wa", "seq"))


def on_device(
    tokens,
    cotangent,
    input_gain,
    gate_proj,
    mixed_proj,
    step_proj,
    conv_kernel,
    conv_bias,
    step_bias,
    decay_log,
    skip_gain,
    output_gain,
    out_proj,
):
    shards = (
        input_gain,
        gate_proj,
        mixed_proj,
        step_proj,
        conv_kernel,
        conv_bias,
        step_bias,
        decay_log,
        skip_gain,
        output_gain,
        out_proj,
    )
    sections = lax.axis_size("section")
    rank = lax.axis_index("section")
    wa_rank = lax.axis_index("wa")
    micro_count = tokens.shape[0]
    share = micro_count // sections
    small = fetch_small(shards)
    large = fetch_large(shards)
    params = []
    for level in range(sections):
        merged = {**small[level], **large[level]}
        params.append(tuple(merged[at] for at in range(len(shards))))

    totals = [None] * sections
    outs = [[None] * share for _ in range(sections)]
    backs = [[None] * share for _ in range(sections)]
    for turn in range(share):
        own = rank * share + turn
        hidden = lax.dynamic_index_in_dim(tokens[:, 0], own, 0, False).astype(jnp.float32)
        tapes = []
        for level in range(sections):
            result, tape = layer_pass(hidden, params[level])
            tapes.append(tape)
            low = result.astype(jnp.bfloat16)
            outs[level][turn] = low
            hidden = low.astype(jnp.float32)
        grad = lax.dynamic_index_in_dim(cotangent[:, 0], own, 0, False).astype(jnp.float32)
        for level in reversed(range(sections)):
            grad, grads = layer_back(grad, params[level], tapes[level])
            backs[level][turn] = grad
            if totals[level] is None:
                totals[level] = grads
            else:
                totals[level] = tuple(a + b for a, b in zip(totals[level], grads))

    layer_out = gather_micro(outs, rank, sections, share)[None, :, None]
    input_grad = gather_micro(backs, rank, sections, share)[None, :, None]

    final = {}
    parts = [None] * sections
    sums = [None] * sections
    before = None
    for level in reversed(range(sections)):
        scattered = tuple(scatter_large(totals[level][at]) for at in LARGE)
        if before is not None:
            scattered, before = lax.optimization_barrier((scattered, before))
            parts[level + 1] = before
        before = lax.psum(scattered, "seq")
        parts[level] = before
        sums[level] = reduce_small(totals[level])
    parts = [dict(zip(LARGE, part)) for part in parts]
    for at in LARGE:
        stacked = jnp.stack([parts[level][at] for level in range(sections)])
        got = swapped(stacked, rank, sections)
        final[at] = jnp.concatenate(got, axis=0).astype(jnp.float32)[None]
    flat = lax.dynamic_index_in_dim(jnp.stack(sums), rank, 0, False)
    start = 0
    for at, axis in SMALL:
        shape = totals[0][at].shape
        size = totals[0][at].size
        whole = flat[start : start + size].reshape(shape)
        start += size
        length = shards[at].shape[axis]
        final[at] = lax.dynamic_slice_in_dim(whole, wa_rank * length, length, axis - 1)[None]
    return (layer_out, input_grad) + tuple(final[at] for at in range(len(shards)))


def gather_micro(values, rank, sections, share):
    stacked = jnp.stack([jnp.stack(rows) for rows in values])
    arrivals = [lax.dynamic_index_in_dim(stacked, rank, 0, False)]
    for hop in range(1, sections):
        target = lax.rem(rank + hop, sections)
        block = lax.dynamic_index_in_dim(stacked, target, 0, False).astype(jnp.bfloat16)
        arrivals.append(
            lax.ppermute(
                block, "section", [(i, (i + hop) % sections) for i in range(sections)]
            ).astype(stacked.dtype)
        )
    pieces = []
    for source in range(sections):
        value = arrivals[0]
        for hop in range(1, sections):
            value = jnp.where(lax.rem(source + hop, sections) == rank, arrivals[hop], value)
        pieces.append(value)
    return jnp.concatenate(pieces, axis=0)


def solution(mesh):
    placed = (
        P(None, "wa", "seq", None),
        P(None, "wa", "seq", None),
        P("section", "wa"),
        P("section", "wa", None),
        P("section", "wa", None),
        P("section", "wa", None),
        P("section", None, "wa"),
        P("section", "wa"),
        P("section", "wa"),
        P("section", "wa"),
        P("section", "wa"),
        P("section", "wa"),
        P("section", "wa", None),
    )
    return jax.shard_map(
        on_device,
        mesh=mesh,
        in_specs=placed,
        out_specs=(
            P("section", None, "wa", "seq", None),
            P("section", None, "wa", "seq", None),
            P("section", "wa"),
            P("section", "wa", None),
            P("section", "wa", None),
            P("section", "wa", None),
            P("section", None, "wa"),
            P("section", "wa"),
            P("section", "wa"),
            P("section", "wa"),
            P("section", "wa"),
            P("section", "wa"),
            P("section", "wa", None),
        ),
        check_vma=False,
    )
```

```python
import jax
import jax.numpy as jnp
from jax import lax
from jax.sharding import PartitionSpec as P

HEADDIM = 64
GROUP = 128


EPSILON = 1e-05
HIGHEST = lax.Precision.DEFAULT


def passed_along(block, axis, distance):
    devices = range(lax.axis_size(axis))
    route = [(i - distance, i) for i in devices if i - distance in devices]
    return lax.ppermute(block, axis, route)


def rms_scale(values, gain):
    return values * lax.rsqrt(jnp.mean(values * values, axis=-1, keepdims=True) + EPSILON) * gain


def expand_heads(decays):
    return jnp.repeat(decays, HEADDIM, axis=-1)[..., None]


def join_states(earlier, later):
    return (earlier[0] * later[0], earlier[1] * expand_heads(later[0]) + later[1])


def entry_piece(hidden, input_gain):
    return rms_scale(hidden, input_gain)


def conv_piece(extended, step_raw, conv_kernel, conv_bias, step_bias, decay_log):
    length = step_raw.shape[0]
    conv_sum = conv_bias
    for offset in range(conv_kernel.shape[0]):
        conv_sum = conv_sum + conv_kernel[offset] * extended[offset : offset + length]
    time_step = jax.nn.softplus(step_raw + step_bias)
    return (jax.nn.silu(conv_sum), time_step, -jnp.exp(decay_log) * time_step)


def block_piece(log_decay, time_step, values, keys_in, queries):
    length = log_decay.shape[0]
    cumulative = jnp.cumsum(log_decay, axis=0)
    gram_mat = jnp.einsum("tn,sn->ts", queries, keys_in, precision=HIGHEST)
    by_head = cumulative.T
    spread = by_head[:, :, None] - by_head[:, None, :]
    lower_mask = (jnp.arange(length)[:, None] >= jnp.arange(length)[None, :])[None]
    decay_mat = jnp.where(lower_mask, jnp.exp(jnp.where(lower_mask, spread, 0.0)), 0.0)
    mixing = gram_mat[None] * decay_mat * time_step.T[:, None, :]
    weight = jnp.exp(cumulative[-1:] - cumulative) * time_step
    scaled = values * jnp.repeat(weight, HEADDIM, axis=1)
    fresh_state = jnp.einsum("sd,sn->dn", scaled, keys_in, precision=HIGHEST)
    return (mixing, fresh_state, jnp.exp(cumulative[-1]), jnp.exp(cumulative))


def reach_piece(growth, queries, start_state):
    reach_mat = jnp.einsum("tn,dn->td", queries, start_state, precision=HIGHEST)
    return reach_mat * jnp.repeat(growth, HEADDIM, axis=1)


def own_piece(fresh_all, decay_all):
    own_state = jnp.zeros_like(fresh_all[0])
    own_decay = jnp.ones_like(decay_all[0])
    prefixes = []
    prefix_decay = []
    for block_index in range(fresh_all.shape[0]):
        prefixes.append(own_state)
        prefix_decay.append(own_decay)
        own_state = own_state * expand_heads(decay_all[block_index]) + fresh_all[block_index]
        own_decay = own_decay * decay_all[block_index]
    return (own_state, own_decay, jnp.stack(prefixes), jnp.stack(prefix_decay))


def start_piece(incoming, prefix_decay, prefixes):
    return incoming[None] * expand_heads(prefix_decay) + prefixes


def exit_piece(inner_all, outer_all, values, skip_gain, gate_pre, output_gain):
    mixed_out = inner_all + outer_all + values * jnp.repeat(skip_gain, HEADDIM)
    return rms_scale(mixed_out * jax.nn.silu(gate_pre), output_gain)


def to_other(block):
    count = lax.axis_size("section")
    return lax.ppermute(block, "section", [(i, (i + 1) % count) for i in range(count)])


def spread_states(state, decay):
    high = decay.astype(jnp.bfloat16)
    low = (decay - high.astype(jnp.float32)).astype(jnp.bfloat16)
    width = state.shape[1]
    heads = decay.shape[0]
    row = jnp.concatenate([high, low, jnp.zeros((width - 2 * heads,), jnp.bfloat16)])[None]
    packed = jnp.concatenate(
        [state.astype(jnp.bfloat16), row, jnp.zeros((15, width), jnp.bfloat16)], axis=0
    )
    gathered = lax.all_gather(packed, "seq")
    states = gathered[:, : state.shape[0]]
    parts = gathered[:, state.shape[0], : 2 * heads].astype(jnp.float32)
    return states, parts[:, :heads] + parts[:, heads:]


def carried_from(states, decays, ahead):
    count = lax.axis_size("seq")
    place = lax.axis_index("seq")
    source = jnp.arange(count)[:, None, None]
    middle = jnp.arange(count)[None, :, None]
    if ahead:
        between = jnp.logical_and(middle < source, middle > place)
        keep = jnp.arange(count) > place
    else:
        between = jnp.logical_and(middle > source, middle < place)
        keep = jnp.arange(count) < place
    factor = jnp.prod(jnp.where(between, decays[None], 1.0), axis=1)
    factor = jnp.where(keep[:, None], factor, 0.0)
    factor = jnp.repeat(factor, HEADDIM, axis=1)
    total = states[0].astype(jnp.float32) * factor[0][:, None]
    for index in range(1, count):
        total = total + states[index].astype(jnp.float32) * factor[index][:, None]
    return total


def layer_pass(hidden, params):
    (
        input_gain,
        gate_proj,
        mixed_proj,
        step_proj,
        conv_kernel,
        conv_bias,
        step_bias,
        decay_log,
        skip_gain,
        output_gain,
        out_proj,
    ) = params
    length = hidden.shape[0]
    inner_width = gate_proj.shape[1]
    state_width = (mixed_proj.shape[1] - inner_width) // 2
    head_count = step_proj.shape[1]
    block_count = length // GROUP
    rim_rows = conv_kernel.shape[0] - 1
    normed, entry_back = jax.vjp(entry_piece, hidden, input_gain.astype(jnp.float32))
    normed_low = normed.astype(jnp.bfloat16)
    gate_pre = jnp.dot(normed_low, gate_proj, preferred_element_type=jnp.float32)
    mixed_low = jnp.dot(normed_low, mixed_proj, preferred_element_type=jnp.float32).astype(
        jnp.bfloat16
    )
    step_raw = jnp.dot(normed_low, step_proj, preferred_element_type=jnp.float32)
    rim_in = passed_along(mixed_low[length - rim_rows :], "seq", 1)
    extended = jnp.concatenate([rim_in, mixed_low], axis=0).astype(jnp.float32)
    conv_out, conv_back = jax.vjp(
        conv_piece,
        extended,
        step_raw,
        conv_kernel.astype(jnp.float32),
        conv_bias.astype(jnp.float32),
        step_bias.astype(jnp.float32),
        decay_log.astype(jnp.float32),
    )
    active, time_step, log_decay = conv_out
    active_low = active.astype(jnp.bfloat16)
    active_up = active_low.astype(jnp.float32)
    values_low = active_low[:, :inner_width]
    values_up = active_up[:, :inner_width]
    keys_up = active_up[:, inner_width : inner_width + state_width]
    queries_up = active_up[:, inner_width + state_width :]
    inner_parts = []
    mixing_list = []
    block_backs = []
    fresh_list = []
    decay_list = []
    growth_list = []
    for block_index in range(block_count):
        row_span = slice(block_index * GROUP, (block_index + 1) * GROUP)
        outputs, block_back = jax.vjp(
            block_piece,
            log_decay[row_span],
            time_step[row_span],
            values_up[row_span],
            keys_up[row_span],
            queries_up[row_span],
        )
        mixing_low = outputs[0].astype(jnp.bfloat16)
        heads_view = values_low[row_span].reshape(GROUP, head_count, HEADDIM)
        inner_parts.append(
            jnp.einsum(
                "hts,shp->thp", mixing_low, heads_view, preferred_element_type=jnp.float32
            ).reshape(GROUP, inner_width)
        )
        mixing_list.append(mixing_low)
        block_backs.append(block_back)
        fresh_list.append(outputs[1])
        decay_list.append(outputs[2])
        growth_list.append(outputs[3])
    own_out, own_back = jax.vjp(own_piece, jnp.stack(fresh_list), jnp.stack(decay_list))
    own_state, own_decay, prefixes, prefix_decay = own_out
    states_all, decays_all = spread_states(own_state, own_decay)
    incoming = carried_from(states_all, decays_all, False)
    starts, start_back = jax.vjp(start_piece, incoming, prefix_decay, prefixes)
    outer_parts = []
    reach_backs = []
    for block_index in range(block_count):
        row_span = slice(block_index * GROUP, (block_index + 1) * GROUP)
        outer_part, reach_back = jax.vjp(
            reach_piece, growth_list[block_index], queries_up[row_span], starts[block_index]
        )
        outer_parts.append(outer_part)
        reach_backs.append(reach_back)
    inner_all = jnp.concatenate(inner_parts, axis=0)
    outer_all = jnp.concatenate(outer_parts, axis=0)
    normed_out, exit_back = jax.vjp(
        exit_piece,
        inner_all,
        outer_all,
        values_up,
        skip_gain.astype(jnp.float32),
        gate_pre,
        output_gain.astype(jnp.float32),
    )
    normed_out_low = normed_out.astype(jnp.bfloat16)
    result = hidden + jnp.dot(normed_out_low, out_proj, preferred_element_type=jnp.float32)
    tape = (
        normed_low,
        entry_back,
        conv_back,
        values_low,
        mixing_list,
        block_backs,
        own_back,
        decays_all,
        incoming,
        start_back,
        reach_backs,
        exit_back,
        normed_out_low,
    )
    return (result, tape)


def layer_back(grad_out, params, tape):
    (
        input_gain,
        gate_proj,
        mixed_proj,
        step_proj,
        conv_kernel,
        conv_bias,
        step_bias,
        decay_log,
        skip_gain,
        output_gain,
        out_proj,
    ) = params
    (
        normed_low,
        entry_back,
        conv_back,
        values_low,
        mixing_list,
        block_backs,
        own_back,
        decays_all,
        incoming,
        start_back,
        reach_backs,
        exit_back,
        normed_out_low,
    ) = tape
    length = grad_out.shape[0]
    inner_width = gate_proj.shape[1]
    head_count = step_proj.shape[1]
    block_count = length // GROUP
    rim_rows = conv_kernel.shape[0] - 1
    grad_proj = grad_out.astype(jnp.bfloat16)
    out_proj_grad = jnp.einsum(
        "te,td->ed", normed_out_low, grad_proj, preferred_element_type=jnp.float32
    )
    grad_normed_out = jnp.einsum(
        "td,ed->te", grad_proj, out_proj, preferred_element_type=jnp.float32
    )
    grad_inner, grad_outer, grad_values_skip, skip_gain_grad, grad_gate_pre, output_gain_grad = (
        exit_back(grad_normed_out)
    )
    grad_gate_low = grad_gate_pre.astype(jnp.bfloat16)
    gate_proj_grad = jnp.einsum(
        "td,te->de", normed_low, grad_gate_low, preferred_element_type=jnp.float32
    )
    grad_inner, grad_outer, grad_values_skip, out_proj_grad, gate_proj_grad = (
        lax.optimization_barrier(
            (
                grad_inner,
                grad_outer,
                grad_values_skip,
                out_proj_grad.astype(jnp.bfloat16),
                gate_proj_grad.astype(jnp.bfloat16),
            )
        )
    )
    grad_inner_low = grad_inner.astype(jnp.bfloat16)
    grad_mixings = []
    grad_values_inner = []
    grad_growths = []
    grad_queries_outer = []
    grad_starts = []
    for block_index in range(block_count):
        row_span = slice(block_index * GROUP, (block_index + 1) * GROUP)
        grad_heads = grad_inner_low[row_span].reshape(GROUP, head_count, HEADDIM)
        heads_view = values_low[row_span].reshape(GROUP, head_count, HEADDIM)
        grad_mixings.append(
            jnp.einsum("thp,shp->hts", grad_heads, heads_view, preferred_element_type=jnp.float32)
        )
        grad_values_inner.append(
            jnp.einsum(
                "hts,thp->shp",
                mixing_list[block_index],
                grad_heads,
                preferred_element_type=jnp.float32,
            ).reshape(GROUP, inner_width)
        )
        grad_growth, grad_query, grad_start = reach_backs[block_index](grad_outer[row_span])
        grad_growths.append(grad_growth)
        grad_queries_outer.append(grad_query)
        grad_starts.append(grad_start)
    grad_incoming, grad_prefix_decay, grad_prefixes = start_back(jnp.stack(grad_starts))
    adjoints = lax.all_gather(grad_incoming.astype(jnp.bfloat16), "seq")
    returned = carried_from(adjoints, decays_all, True)
    grad_own_decay = jnp.sum(returned * incoming, axis=1).reshape(head_count, HEADDIM).sum(axis=1)
    grad_fresh, grad_decays = own_back((returned, grad_own_decay, grad_prefixes, grad_prefix_decay))
    grad_log_list = []
    grad_step_list = []
    grad_values_list = []
    grad_keys_list = []
    grad_queries_list = []
    for block_index in range(block_count):
        grad_log, grad_step, grad_values, grad_keys, grad_queries = block_backs[block_index](
            (
                grad_mixings[block_index],
                grad_fresh[block_index],
                grad_decays[block_index],
                grad_growths[block_index],
            )
        )
        grad_log_list.append(grad_log)
        grad_step_list.append(grad_step)
        grad_values_list.append(grad_values + grad_values_inner[block_index])
        grad_keys_list.append(grad_keys)
        grad_queries_list.append(grad_queries + grad_queries_outer[block_index])
    grad_active = jnp.concatenate(
        [
            jnp.concatenate(grad_values_list, axis=0) + grad_values_skip,
            jnp.concatenate(grad_keys_list, axis=0),
            jnp.concatenate(grad_queries_list, axis=0),
        ],
        axis=1,
    )
    (
        grad_extended,
        grad_step_raw,
        conv_kernel_grad,
        conv_bias_grad,
        step_bias_grad,
        decay_log_grad,
    ) = conv_back(
        (
            grad_active,
            jnp.concatenate(grad_step_list, axis=0),
            jnp.concatenate(grad_log_list, axis=0),
        )
    )
    back_rim = passed_along(grad_extended[:rim_rows], "seq", -1)
    grad_mixed = grad_extended[rim_rows:] + jnp.pad(back_rim, ((length - rim_rows, 0), (0, 0)))
    grad_mixed_low = grad_mixed.astype(jnp.bfloat16)
    grad_step_low = grad_step_raw.astype(jnp.bfloat16)
    mixed_proj_grad = jnp.einsum(
        "td,te->de", normed_low, grad_mixed_low, preferred_element_type=jnp.float32
    ).astype(jnp.bfloat16)
    step_proj_grad = jnp.einsum(
        "td,te->de", normed_low, grad_step_low, preferred_element_type=jnp.float32
    )
    grad_normed = jnp.einsum(
        "te,de->td", grad_gate_low, gate_proj, preferred_element_type=jnp.float32
    )
    grad_normed = grad_normed + jnp.einsum(
        "te,de->td", grad_mixed_low, mixed_proj, preferred_element_type=jnp.float32
    )
    grad_normed = grad_normed + jnp.einsum(
        "te,de->td", grad_step_low, step_proj, preferred_element_type=jnp.float32
    )
    grad_hidden, input_gain_grad = entry_back(grad_normed)
    grads = (
        input_gain_grad,
        gate_proj_grad,
        mixed_proj_grad,
        step_proj_grad,
        conv_kernel_grad,
        conv_bias_grad,
        step_bias_grad,
        decay_log_grad,
        skip_gain_grad,
        output_gain_grad,
        out_proj_grad,
    )
    return (grad_out + grad_hidden, grads)


SMALL = ((0, 1), (3, 1), (4, 2), (5, 1), (6, 1), (7, 1), (8, 1), (9, 1))
LARGE = (2, 1, 10)


def fetch_small(shards):
    flat = jnp.concatenate([shards[at].reshape(-1) for at, _ in SMALL])
    flat = jnp.pad(flat, (0, -flat.shape[0] % 2048)).reshape(-1, 128)
    gathered = lax.all_gather(flat, ("wa", "section"), axis=0, tiled=True)
    sections = lax.axis_size("section")
    count = lax.axis_size("wa")
    gathered = jnp.moveaxis(gathered.reshape(count, sections, -1), 1, 0)
    layers = []
    for level in range(sections):
        whole = {}
        start = 0
        for at, axis in SMALL:
            shape = shards[at].shape[1:]
            size = shards[at][0].size
            part = gathered[level, :, start : start + size]
            start += size
            part = part.reshape((count,) + shape)
            if axis == 1:
                whole[at] = part.reshape((count * shape[0],) + shape[1:])
            else:
                whole[at] = jnp.moveaxis(part, 0, 1).reshape((shape[0], count * shape[1]))
        layers.append(whole)
    return layers


def fetch_large(shards):
    sections = lax.axis_size("section")
    rank = lax.axis_index("section")
    mine = {at: shards[at][0] for at in LARGE}
    layers = [dict() for _ in range(sections)]
    for at in LARGE:
        rows, columns = mine[at].shape
        cut = mine[at].reshape(sections, rows // sections, columns)
        pieces = swapped(cut, rank, sections)
        for level in range(sections):
            layers[level][at] = lax.all_gather(
                pieces[level], ("wa", "section"), axis=0, tiled=True
            )
    return layers


def swapped(cut, rank, sections):
    got = [None] * sections
    arrivals = [lax.dynamic_index_in_dim(cut, rank, 0, False)]
    for hop in range(1, sections):
        target = lax.rem(rank + hop, sections)
        block = lax.dynamic_index_in_dim(cut, target, 0, False)
        arrivals.append(
            lax.ppermute(block, "section", [(i, (i + hop) % sections) for i in range(sections)])
        )
    for level in range(sections):
        value = arrivals[0]
        for hop in range(1, sections):
            value = jnp.where(lax.rem(level + hop, sections) == rank, arrivals[hop], value)
        got[level] = value
    return got


def scatter_large(grad):
    sections = lax.axis_size("section")
    rank = lax.axis_index("section")
    count = lax.axis_size("wa")
    rows, columns = grad.shape
    cut = grad.reshape(count, sections, rows // (count * sections), columns)
    total = lax.dynamic_index_in_dim(cut, rank, 1, False).astype(jnp.float32)
    for hop in range(1, sections):
        block = lax.dynamic_index_in_dim(cut, lax.rem(rank + hop, sections), 1, False)
        came = lax.ppermute(block, "section", [(i, (i + hop) % sections) for i in range(sections)])
        total = total + came.astype(jnp.float32)
    total = total.astype(jnp.bfloat16).reshape(rows // sections, columns)
    return lax.psum_scatter(total, "wa", scatter_dimension=0, tiled=True)


def on_device(
    tokens,
    cotangent,
    input_gain,
    gate_proj,
    mixed_proj,
    step_proj,
    conv_kernel,
    conv_bias,
    step_bias,
    decay_log,
    skip_gain,
    output_gain,
    out_proj,
):
    shards = (
        input_gain,
        gate_proj,
        mixed_proj,
        step_proj,
        conv_kernel,
        conv_bias,
        step_bias,
        decay_log,
        skip_gain,
        output_gain,
        out_proj,
    )
    sections = lax.axis_size("section")
    rank = lax.axis_index("section")
    wa_rank = lax.axis_index("wa")
    micro_count = tokens.shape[0]
    share = micro_count // sections
    small = fetch_small(shards)
    large = fetch_large(shards)
    params = []
    for level in range(sections):
        merged = {**small[level], **large[level]}
        params.append(tuple(merged[at] for at in range(len(shards))))

    totals = [None] * sections
    outs = [[None] * share for _ in range(sections)]
    backs = [[None] * share for _ in range(sections)]
    for turn in range(share):
        own = rank * share + turn
        hidden = lax.dynamic_index_in_dim(tokens[:, 0], own, 0, False).astype(jnp.float32)
        tapes = []
        for level in range(sections):
            result, tape = layer_pass(hidden, params[level])
            tapes.append(tape)
            low = result.astype(jnp.bfloat16)
            outs[level][turn] = low
            hidden = low.astype(jnp.float32)
        grad = lax.dynamic_index_in_dim(cotangent[:, 0], own, 0, False).astype(jnp.float32)
        for level in reversed(range(sections)):
            grad, grads = layer_back(grad, params[level], tapes[level])
            grad, grads = lax.optimization_barrier((grad, grads))
            backs[level][turn] = grad
            if totals[level] is None:
                totals[level] = grads
            else:
                totals[level] = tuple(
                    (a.astype(jnp.float32) + b.astype(jnp.float32)).astype(a.dtype)
                    for a, b in zip(totals[level], grads)
                )

    layer_out = gather_micro(outs, rank, sections, share)[None, :, None]
    input_grad = gather_micro(backs, rank, sections, share)[None, :, None]

    final = {}
    parts = [dict() for _ in range(sections)]
    sums = [None] * sections
    before = None
    sum_before = None
    for level in reversed(range(sections)):
        for at in (10, 1, 2):
            scattered = scatter_large(totals[level][at])
            if before is not None:
                scattered, parts[before[0]][before[1]] = lax.optimization_barrier(
                    (scattered, parts[before[0]][before[1]])
                )
            parts[level][at] = lax.psum(scattered, "seq")
            before = (level, at)
        flat = jnp.concatenate([totals[level][at].reshape(-1) for at, _ in SMALL])
        if sum_before is not None:
            flat, sums[sum_before] = lax.optimization_barrier((flat, sums[sum_before]))
        sums[level] = lax.psum(flat, ("section", "wa", "seq"))
        sum_before = level
    for at in LARGE:
        stacked = jnp.stack([parts[level][at] for level in range(sections)])
        got = swapped(stacked, rank, sections)
        final[at] = jnp.concatenate(got, axis=0).astype(jnp.float32)[None]
    flat = lax.dynamic_index_in_dim(jnp.stack(sums), rank, 0, False)
    start = 0
    for at, axis in SMALL:
        shape = totals[0][at].shape
        size = totals[0][at].size
        whole = flat[start : start + size].reshape(shape)
        start += size
        length = shards[at].shape[axis]
        final[at] = lax.dynamic_slice_in_dim(whole, wa_rank * length, length, axis - 1)[None]
    return (layer_out, input_grad) + tuple(final[at] for at in range(len(shards)))


def gather_micro(values, rank, sections, share):
    stacked = jnp.stack([jnp.stack(rows) for rows in values])
    arrivals = [lax.dynamic_index_in_dim(stacked, rank, 0, False)]
    for hop in range(1, sections):
        target = lax.rem(rank + hop, sections)
        block = lax.dynamic_index_in_dim(stacked, target, 0, False).astype(jnp.bfloat16)
        arrivals.append(
            lax.ppermute(
                block, "section", [(i, (i + hop) % sections) for i in range(sections)]
            ).astype(stacked.dtype)
        )
    pieces = []
    for source in range(sections):
        value = arrivals[0]
        for hop in range(1, sections):
            value = jnp.where(lax.rem(source + hop, sections) == rank, arrivals[hop], value)
        pieces.append(value)
    return jnp.concatenate(pieces, axis=0)


def solution(mesh):
    placed = (
        P(None, "wa", "seq", None),
        P(None, "wa", "seq", None),
        P("section", "wa"),
        P("section", "wa", None),
        P("section", "wa", None),
        P("section", "wa", None),
        P("section", None, "wa"),
        P("section", "wa"),
        P("section", "wa"),
        P("section", "wa"),
        P("section", "wa"),
        P("section", "wa"),
        P("section", "wa", None),
    )
    return jax.shard_map(
        on_device,
        mesh=mesh,
        in_specs=placed,
        out_specs=(
            P("section", None, "wa", "seq", None),
            P("section", None, "wa", "seq", None),
            P("section", "wa"),
            P("section", "wa", None),
            P("section", "wa", None),
            P("section", "wa", None),
            P("section", None, "wa"),
            P("section", "wa"),
            P("section", "wa"),
            P("section", "wa"),
            P("section", "wa"),
            P("section", "wa"),
            P("section", "wa", None),
        ),
        check_vma=False,
    )
```

```python
import jax
import jax.numpy as jnp
from jax import lax
from jax.sharding import PartitionSpec as P

HEADDIM = 64
GROUP = 128


EPSILON = 1e-05
HIGHEST = lax.Precision.DEFAULT


def passed_along(block, axis, distance):
    devices = range(lax.axis_size(axis))
    route = [(i - distance, i) for i in devices if i - distance in devices]
    return lax.ppermute(block, axis, route)


def rms_scale(values, gain):
    return values * lax.rsqrt(jnp.mean(values * values, axis=-1, keepdims=True) + EPSILON) * gain


def expand_heads(decays):
    return jnp.repeat(decays, HEADDIM, axis=-1)[..., None]


def join_states(earlier, later):
    return (earlier[0] * later[0], earlier[1] * expand_heads(later[0]) + later[1])


def entry_piece(hidden, input_gain):
    return rms_scale(hidden, input_gain)


def conv_piece(extended, step_raw, conv_kernel, conv_bias, step_bias, decay_log):
    length = step_raw.shape[0]
    conv_sum = conv_bias
    for offset in range(conv_kernel.shape[0]):
        conv_sum = conv_sum + conv_kernel[offset] * extended[offset : offset + length]
    time_step = jax.nn.softplus(step_raw + step_bias)
    return (jax.nn.silu(conv_sum), time_step, -jnp.exp(decay_log) * time_step)


def block_piece(log_decay, time_step, values, keys_in, queries):
    length = log_decay.shape[0]
    cumulative = jnp.cumsum(log_decay, axis=0)
    gram_mat = jnp.einsum("tn,sn->ts", queries, keys_in, precision=HIGHEST)
    by_head = cumulative.T
    spread = by_head[:, :, None] - by_head[:, None, :]
    lower_mask = (jnp.arange(length)[:, None] >= jnp.arange(length)[None, :])[None]
    decay_mat = jnp.where(lower_mask, jnp.exp(jnp.where(lower_mask, spread, 0.0)), 0.0)
    mixing = gram_mat[None] * decay_mat * time_step.T[:, None, :]
    weight = jnp.exp(cumulative[-1:] - cumulative) * time_step
    scaled = values * jnp.repeat(weight, HEADDIM, axis=1)
    fresh_state = jnp.einsum("sd,sn->dn", scaled, keys_in, precision=HIGHEST)
    return (mixing, fresh_state, jnp.exp(cumulative[-1]), jnp.exp(cumulative))


def reach_piece(growth, queries, start_state):
    reach_mat = jnp.einsum("tn,dn->td", queries, start_state, precision=HIGHEST)
    return reach_mat * jnp.repeat(growth, HEADDIM, axis=1)


def own_piece(fresh_all, decay_all):
    own_state = jnp.zeros_like(fresh_all[0])
    own_decay = jnp.ones_like(decay_all[0])
    prefixes = []
    prefix_decay = []
    for block_index in range(fresh_all.shape[0]):
        prefixes.append(own_state)
        prefix_decay.append(own_decay)
        own_state = own_state * expand_heads(decay_all[block_index]) + fresh_all[block_index]
        own_decay = own_decay * decay_all[block_index]
    return (own_state, own_decay, jnp.stack(prefixes), jnp.stack(prefix_decay))


def start_piece(incoming, prefix_decay, prefixes):
    return incoming[None] * expand_heads(prefix_decay) + prefixes


def exit_piece(inner_all, outer_all, values, skip_gain, gate_pre, output_gain):
    mixed_out = inner_all + outer_all + values * jnp.repeat(skip_gain, HEADDIM)
    return rms_scale(mixed_out * jax.nn.silu(gate_pre), output_gain)


def to_other(block):
    count = lax.axis_size("section")
    return lax.ppermute(block, "section", [(i, (i + 1) % count) for i in range(count)])


def spread_states(state, decay):
    high = decay.astype(jnp.bfloat16)
    low = (decay - high.astype(jnp.float32)).astype(jnp.bfloat16)
    width = state.shape[1]
    heads = decay.shape[0]
    row = jnp.concatenate([high, low, jnp.zeros((width - 2 * heads,), jnp.bfloat16)])[None]
    packed = jnp.concatenate(
        [state.astype(jnp.bfloat16), row, jnp.zeros((15, width), jnp.bfloat16)], axis=0
    )
    gathered = lax.all_gather(packed, "seq")
    states = gathered[:, : state.shape[0]]
    parts = gathered[:, state.shape[0], : 2 * heads].astype(jnp.float32)
    return states, parts[:, :heads] + parts[:, heads:]


def carried_from(states, decays, ahead):
    count = lax.axis_size("seq")
    place = lax.axis_index("seq")
    source = jnp.arange(count)[:, None, None]
    middle = jnp.arange(count)[None, :, None]
    if ahead:
        between = jnp.logical_and(middle < source, middle > place)
        keep = jnp.arange(count) > place
    else:
        between = jnp.logical_and(middle > source, middle < place)
        keep = jnp.arange(count) < place
    factor = jnp.prod(jnp.where(between, decays[None], 1.0), axis=1)
    factor = jnp.where(keep[:, None], factor, 0.0)
    factor = jnp.repeat(factor, HEADDIM, axis=1)
    total = states[0].astype(jnp.float32) * factor[0][:, None]
    for index in range(1, count):
        total = total + states[index].astype(jnp.float32) * factor[index][:, None]
    return total


def layer_pass(hidden, params):
    (
        input_gain,
        gate_proj,
        mixed_proj,
        step_proj,
        conv_kernel,
        conv_bias,
        step_bias,
        decay_log,
        skip_gain,
        output_gain,
        out_proj,
    ) = params
    length = hidden.shape[0]
    inner_width = gate_proj.shape[1]
    state_width = (mixed_proj.shape[1] - inner_width) // 2
    head_count = step_proj.shape[1]
    block_count = length // GROUP
    rim_rows = conv_kernel.shape[0] - 1
    normed, entry_back = jax.vjp(entry_piece, hidden, input_gain.astype(jnp.float32))
    normed_low = normed.astype(jnp.bfloat16)
    gate_pre = jnp.dot(normed_low, gate_proj, preferred_element_type=jnp.float32)
    mixed_low = jnp.dot(normed_low, mixed_proj, preferred_element_type=jnp.float32).astype(
        jnp.bfloat16
    )
    step_raw = jnp.dot(normed_low, step_proj, preferred_element_type=jnp.float32)
    rim_in = passed_along(mixed_low[length - rim_rows :], "seq", 1)
    extended = jnp.concatenate([rim_in, mixed_low], axis=0).astype(jnp.float32)
    conv_out, conv_back = jax.vjp(
        conv_piece,
        extended,
        step_raw,
        conv_kernel.astype(jnp.float32),
        conv_bias.astype(jnp.float32),
        step_bias.astype(jnp.float32),
        decay_log.astype(jnp.float32),
    )
    active, time_step, log_decay = conv_out
    active_low = active.astype(jnp.bfloat16)
    active_up = active_low.astype(jnp.float32)
    values_low = active_low[:, :inner_width]
    values_up = active_up[:, :inner_width]
    keys_up = active_up[:, inner_width : inner_width + state_width]
    queries_up = active_up[:, inner_width + state_width :]
    inner_parts = []
    mixing_list = []
    block_backs = []
    fresh_list = []
    decay_list = []
    growth_list = []
    for block_index in range(block_count):
        row_span = slice(block_index * GROUP, (block_index + 1) * GROUP)
        outputs, block_back = jax.vjp(
            block_piece,
            log_decay[row_span],
            time_step[row_span],
            values_up[row_span],
            keys_up[row_span],
            queries_up[row_span],
        )
        mixing_low = outputs[0].astype(jnp.bfloat16)
        heads_view = values_low[row_span].reshape(GROUP, head_count, HEADDIM)
        inner_parts.append(
            jnp.einsum(
                "hts,shp->thp", mixing_low, heads_view, preferred_element_type=jnp.float32
            ).reshape(GROUP, inner_width)
        )
        mixing_list.append(mixing_low)
        block_backs.append(block_back)
        fresh_list.append(outputs[1])
        decay_list.append(outputs[2])
        growth_list.append(outputs[3])
    own_out, own_back = jax.vjp(own_piece, jnp.stack(fresh_list), jnp.stack(decay_list))
    own_state, own_decay, prefixes, prefix_decay = own_out
    states_all, decays_all = spread_states(own_state, own_decay)
    incoming = carried_from(states_all, decays_all, False)
    starts, start_back = jax.vjp(start_piece, incoming, prefix_decay, prefixes)
    outer_parts = []
    reach_backs = []
    for block_index in range(block_count):
        row_span = slice(block_index * GROUP, (block_index + 1) * GROUP)
        outer_part, reach_back = jax.vjp(
            reach_piece, growth_list[block_index], queries_up[row_span], starts[block_index]
        )
        outer_parts.append(outer_part)
        reach_backs.append(reach_back)
    inner_all = jnp.concatenate(inner_parts, axis=0)
    outer_all = jnp.concatenate(outer_parts, axis=0)
    normed_out, exit_back = jax.vjp(
        exit_piece,
        inner_all,
        outer_all,
        values_up,
        skip_gain.astype(jnp.float32),
        gate_pre,
        output_gain.astype(jnp.float32),
    )
    normed_out_low = normed_out.astype(jnp.bfloat16)
    result = hidden + jnp.dot(normed_out_low, out_proj, preferred_element_type=jnp.float32)
    tape = (
        normed_low,
        entry_back,
        conv_back,
        values_low,
        mixing_list,
        block_backs,
        own_back,
        decays_all,
        incoming,
        start_back,
        reach_backs,
        exit_back,
        normed_out_low,
    )
    return (result, tape)


def layer_back(grad_out, params, tape):
    (
        input_gain,
        gate_proj,
        mixed_proj,
        step_proj,
        conv_kernel,
        conv_bias,
        step_bias,
        decay_log,
        skip_gain,
        output_gain,
        out_proj,
    ) = params
    (
        normed_low,
        entry_back,
        conv_back,
        values_low,
        mixing_list,
        block_backs,
        own_back,
        decays_all,
        incoming,
        start_back,
        reach_backs,
        exit_back,
        normed_out_low,
    ) = tape
    length = grad_out.shape[0]
    inner_width = gate_proj.shape[1]
    head_count = step_proj.shape[1]
    block_count = length // GROUP
    rim_rows = conv_kernel.shape[0] - 1
    grad_proj = grad_out.astype(jnp.bfloat16)
    out_proj_grad = jnp.einsum(
        "te,td->ed", normed_out_low, grad_proj, preferred_element_type=jnp.float32
    )
    grad_normed_out = jnp.einsum(
        "td,ed->te", grad_proj, out_proj, preferred_element_type=jnp.float32
    )
    grad_inner, grad_outer, grad_values_skip, skip_gain_grad, grad_gate_pre, output_gain_grad = (
        exit_back(grad_normed_out)
    )
    grad_gate_low = grad_gate_pre.astype(jnp.bfloat16)
    gate_proj_grad = jnp.einsum(
        "td,te->de", normed_low, grad_gate_low, preferred_element_type=jnp.float32
    )
    grad_inner, grad_outer, grad_values_skip, out_proj_grad, gate_proj_grad = (
        lax.optimization_barrier(
            (
                grad_inner,
                grad_outer,
                grad_values_skip,
                out_proj_grad.astype(jnp.bfloat16),
                gate_proj_grad.astype(jnp.bfloat16),
            )
        )
    )
    grad_inner_low = grad_inner.astype(jnp.bfloat16)
    grad_mixings = []
    grad_values_inner = []
    grad_growths = []
    grad_queries_outer = []
    grad_starts = []
    for block_index in range(block_count):
        row_span = slice(block_index * GROUP, (block_index + 1) * GROUP)
        grad_heads = grad_inner_low[row_span].reshape(GROUP, head_count, HEADDIM)
        heads_view = values_low[row_span].reshape(GROUP, head_count, HEADDIM)
        grad_mixings.append(
            jnp.einsum("thp,shp->hts", grad_heads, heads_view, preferred_element_type=jnp.float32)
        )
        grad_values_inner.append(
            jnp.einsum(
                "hts,thp->shp",
                mixing_list[block_index],
                grad_heads,
                preferred_element_type=jnp.float32,
            ).reshape(GROUP, inner_width)
        )
        grad_growth, grad_query, grad_start = reach_backs[block_index](grad_outer[row_span])
        grad_growths.append(grad_growth)
        grad_queries_outer.append(grad_query)
        grad_starts.append(grad_start)
    grad_incoming, grad_prefix_decay, grad_prefixes = start_back(jnp.stack(grad_starts))
    adjoints = lax.all_gather(grad_incoming.astype(jnp.bfloat16), "seq")
    returned = carried_from(adjoints, decays_all, True)
    grad_own_decay = jnp.sum(returned * incoming, axis=1).reshape(head_count, HEADDIM).sum(axis=1)
    grad_fresh, grad_decays = own_back((returned, grad_own_decay, grad_prefixes, grad_prefix_decay))
    grad_log_list = []
    grad_step_list = []
    grad_values_list = []
    grad_keys_list = []
    grad_queries_list = []
    for block_index in range(block_count):
        grad_log, grad_step, grad_values, grad_keys, grad_queries = block_backs[block_index](
            (
                grad_mixings[block_index],
                grad_fresh[block_index],
                grad_decays[block_index],
                grad_growths[block_index],
            )
        )
        grad_log_list.append(grad_log)
        grad_step_list.append(grad_step)
        grad_values_list.append(grad_values + grad_values_inner[block_index])
        grad_keys_list.append(grad_keys)
        grad_queries_list.append(grad_queries + grad_queries_outer[block_index])
    grad_active = jnp.concatenate(
        [
            jnp.concatenate(grad_values_list, axis=0) + grad_values_skip,
            jnp.concatenate(grad_keys_list, axis=0),
            jnp.concatenate(grad_queries_list, axis=0),
        ],
        axis=1,
    )
    (
        grad_extended,
        grad_step_raw,
        conv_kernel_grad,
        conv_bias_grad,
        step_bias_grad,
        decay_log_grad,
    ) = conv_back(
        (
            grad_active,
            jnp.concatenate(grad_step_list, axis=0),
            jnp.concatenate(grad_log_list, axis=0),
        )
    )
    back_rim = passed_along(grad_extended[:rim_rows], "seq", -1)
    grad_mixed = grad_extended[rim_rows:] + jnp.pad(back_rim, ((length - rim_rows, 0), (0, 0)))
    grad_mixed_low = grad_mixed.astype(jnp.bfloat16)
    grad_step_low = grad_step_raw.astype(jnp.bfloat16)
    mixed_proj_grad = jnp.einsum(
        "td,te->de", normed_low, grad_mixed_low, preferred_element_type=jnp.float32
    ).astype(jnp.bfloat16)
    step_proj_grad = jnp.einsum(
        "td,te->de", normed_low, grad_step_low, preferred_element_type=jnp.float32
    )
    grad_normed = jnp.einsum(
        "te,de->td", grad_gate_low, gate_proj, preferred_element_type=jnp.float32
    )
    grad_normed = grad_normed + jnp.einsum(
        "te,de->td", grad_mixed_low, mixed_proj, preferred_element_type=jnp.float32
    )
    grad_normed = grad_normed + jnp.einsum(
        "te,de->td", grad_step_low, step_proj, preferred_element_type=jnp.float32
    )
    grad_hidden, input_gain_grad = entry_back(grad_normed)
    grads = (
        input_gain_grad,
        gate_proj_grad,
        mixed_proj_grad,
        step_proj_grad,
        conv_kernel_grad,
        conv_bias_grad,
        step_bias_grad,
        decay_log_grad,
        skip_gain_grad,
        output_gain_grad,
        out_proj_grad,
    )
    return (grad_out + grad_hidden, grads)


SMALL = ((0, 1), (3, 1), (4, 2), (5, 1), (6, 1), (7, 1), (8, 1), (9, 1))
LARGE = (2, 1, 10)


def fetch_small(shards):
    flat = jnp.concatenate([shards[at].reshape(-1) for at, _ in SMALL])
    flat = jnp.pad(flat, (0, -flat.shape[0] % 2048)).reshape(-1, 128)
    gathered = lax.all_gather(flat, ("wa", "section"), axis=0, tiled=True)
    sections = lax.axis_size("section")
    count = lax.axis_size("wa")
    gathered = jnp.moveaxis(gathered.reshape(count, sections, -1), 1, 0)
    layers = []
    for level in range(sections):
        whole = {}
        start = 0
        for at, axis in SMALL:
            shape = shards[at].shape[1:]
            size = shards[at][0].size
            part = gathered[level, :, start : start + size]
            start += size
            part = part.reshape((count,) + shape)
            if axis == 1:
                whole[at] = part.reshape((count * shape[0],) + shape[1:])
            else:
                whole[at] = jnp.moveaxis(part, 0, 1).reshape((shape[0], count * shape[1]))
        layers.append(whole)
    return layers


def fetch_large(shards):
    sections = lax.axis_size("section")
    rank = lax.axis_index("section")
    mine = {at: shards[at][0] for at in LARGE}
    layers = [dict() for _ in range(sections)]
    for at in LARGE:
        rows, columns = mine[at].shape
        cut = mine[at].reshape(sections, rows // sections, columns)
        pieces = swapped(cut, rank, sections)
        for level in range(sections):
            layers[level][at] = lax.all_gather(
                pieces[level], ("wa", "section"), axis=0, tiled=True
            )
    return layers


def swapped(cut, rank, sections):
    got = [None] * sections
    arrivals = [lax.dynamic_index_in_dim(cut, rank, 0, False)]
    for hop in range(1, sections):
        target = lax.rem(rank + hop, sections)
        block = lax.dynamic_index_in_dim(cut, target, 0, False)
        arrivals.append(
            lax.ppermute(block, "section", [(i, (i + hop) % sections) for i in range(sections)])
        )
    for level in range(sections):
        value = arrivals[0]
        for hop in range(1, sections):
            value = jnp.where(lax.rem(level + hop, sections) == rank, arrivals[hop], value)
        got[level] = value
    return got


def scatter_large(grad):
    sections = lax.axis_size("section")
    rank = lax.axis_index("section")
    count = lax.axis_size("wa")
    rows, columns = grad.shape
    cut = grad.reshape(count, sections, rows // (count * sections), columns)
    total = lax.dynamic_index_in_dim(cut, rank, 1, False).astype(jnp.float32)
    for hop in range(1, sections):
        block = lax.dynamic_index_in_dim(cut, lax.rem(rank + hop, sections), 1, False)
        came = lax.ppermute(block, "section", [(i, (i + hop) % sections) for i in range(sections)])
        total = total + came.astype(jnp.float32)
    total = total.astype(jnp.bfloat16).reshape(rows // sections, columns)
    return lax.psum_scatter(total, "wa", scatter_dimension=0, tiled=True)


def on_device(
    tokens,
    cotangent,
    input_gain,
    gate_proj,
    mixed_proj,
    step_proj,
    conv_kernel,
    conv_bias,
    step_bias,
    decay_log,
    skip_gain,
    output_gain,
    out_proj,
):
    shards = (
        input_gain,
        gate_proj,
        mixed_proj,
        step_proj,
        conv_kernel,
        conv_bias,
        step_bias,
        decay_log,
        skip_gain,
        output_gain,
        out_proj,
    )
    sections = lax.axis_size("section")
    rank = lax.axis_index("section")
    wa_rank = lax.axis_index("wa")
    micro_count = tokens.shape[0]
    share = micro_count // sections
    small = fetch_small(shards)
    large = fetch_large(shards)
    params = []
    for level in range(sections):
        merged = {**small[level], **large[level]}
        params.append(tuple(merged[at] for at in range(len(shards))))

    totals = [None] * sections
    outs = [[None] * share for _ in range(sections)]
    backs = [[None] * share for _ in range(sections)]
    for turn in range(share):
        own = rank * share + turn
        hidden = lax.dynamic_index_in_dim(tokens[:, 0], own, 0, False).astype(jnp.float32)
        tapes = []
        for level in range(sections):
            result, tape = layer_pass(hidden, params[level])
            tapes.append(tape)
            low = result.astype(jnp.bfloat16)
            outs[level][turn] = low
            hidden = low.astype(jnp.float32)
        grad = lax.dynamic_index_in_dim(cotangent[:, 0], own, 0, False).astype(jnp.float32)
        for level in reversed(range(sections)):
            grad, grads = layer_back(grad, params[level], tapes[level])
            grad, grads = lax.optimization_barrier((grad, grads))
            backs[level][turn] = grad
            if totals[level] is None:
                totals[level] = grads
            else:
                totals[level] = tuple(
                    (a.astype(jnp.float32) + b.astype(jnp.float32)).astype(a.dtype)
                    for a, b in zip(totals[level], grads)
                )

    layer_out = gather_micro(outs, rank, sections, share)[None, :, None]
    input_grad = gather_micro(backs, rank, sections, share)[None, :, None]

    final = {}
    parts = [dict() for _ in range(sections)]
    before = None
    for level in reversed(range(sections)):
        for at in (10, 1, 2):
            scattered = scatter_large(totals[level][at])
            if before is not None:
                scattered, parts[before[0]][before[1]] = lax.optimization_barrier(
                    (scattered, parts[before[0]][before[1]])
                )
            parts[level][at] = lax.psum(scattered, "seq")
            before = (level, at)
    for at in LARGE:
        stacked = jnp.stack([parts[level][at] for level in range(sections)])
        got = swapped(stacked, rank, sections)
        final[at] = jnp.concatenate(got, axis=0).astype(jnp.float32)[None]
    count = lax.axis_size("wa")
    rows = []
    for level in range(sections):
        cuts = []
        for at, axis in SMALL:
            value = totals[level][at]
            if axis == 2:
                value = jnp.moveaxis(value.reshape(value.shape[0], count, -1), 1, 0)
            cuts.append(value.reshape(count, -1))
        row = jnp.concatenate(cuts, axis=1)
        rows.append(jnp.pad(row, ((0, 0), (0, -row.shape[1] % 2048))).reshape(-1, 128))
    got = swapped(jnp.stack(rows), rank, sections)
    mine = got[0]
    for piece in got[1:]:
        mine = mine + piece
    mine = lax.psum_scatter(mine, "wa", scatter_dimension=0, tiled=True)
    flat = lax.psum(mine, "seq").reshape(-1)
    start = 0
    for at, axis in SMALL:
        shape = shards[at].shape
        size = shards[at].size
        final[at] = flat[start : start + size].reshape(shape)
        start += size
    return (layer_out, input_grad) + tuple(final[at] for at in range(len(shards)))


def gather_micro(values, rank, sections, share):
    stacked = jnp.stack([jnp.stack(rows) for rows in values])
    arrivals = [lax.dynamic_index_in_dim(stacked, rank, 0, False)]
    for hop in range(1, sections):
        target = lax.rem(rank + hop, sections)
        block = lax.dynamic_index_in_dim(stacked, target, 0, False).astype(jnp.bfloat16)
        arrivals.append(
            lax.ppermute(
                block, "section", [(i, (i + hop) % sections) for i in range(sections)]
            ).astype(stacked.dtype)
        )
    pieces = []
    for source in range(sections):
        value = arrivals[0]
        for hop in range(1, sections):
            value = jnp.where(lax.rem(source + hop, sections) == rank, arrivals[hop], value)
        pieces.append(value)
    return jnp.concatenate(pieces, axis=0)


def solution(mesh):
    placed = (
        P(None, "wa", "seq", None),
        P(None, "wa", "seq", None),
        P("section", "wa"),
        P("section", "wa", None),
        P("section", "wa", None),
        P("section", "wa", None),
        P("section", None, "wa"),
        P("section", "wa"),
        P("section", "wa"),
        P("section", "wa"),
        P("section", "wa"),
        P("section", "wa"),
        P("section", "wa", None),
    )
    return jax.shard_map(
        on_device,
        mesh=mesh,
        in_specs=placed,
        out_specs=(
            P("section", None, "wa", "seq", None),
            P("section", None, "wa", "seq", None),
            P("section", "wa"),
            P("section", "wa", None),
            P("section", "wa", None),
            P("section", "wa", None),
            P("section", None, "wa"),
            P("section", "wa"),
            P("section", "wa"),
            P("section", "wa"),
            P("section", "wa"),
            P("section", "wa"),
            P("section", "wa", None),
        ),
        check_vma=False,
    )
```
